32 devices in a mesh: group: 2 (over y), expert: 2 (over core), tensor: 8 (over z, x).
Axes of the slice: x: 2, y: 2, z: 4, core: 2. Of those that a mesh axis runs over, the one named last changes fastest.
Arguments:
- tokens: bfloat16 [512, 6144], P(('group', 'expert'), 'tensor'), parts along dimension 0, may hold values from -6 to 6
- routes: int32 [512, 2], P('group'), parts along dimension 0, may hold values from 0 to 3, all different within a row; in each aligned block of 128 rows (0 to 127, 128 to 255, ...) at most 128 rows name the same one
- route_weights: float32 [512, 2], P('group'), parts along dimension 0, may hold values from 0.1 to 0.9
- gate_weight: bfloat16 [4, 8192, 6144], P('expert', 'tensor'), may hold values from -0.078125 to 0.078125
- up_weight: bfloat16 [4, 8192, 6144], P('expert', 'tensor'), may hold values from -0.078125 to 0.078125
- down_weight: bfloat16 [4, 6144, 8192], P('expert', 'tensor'), may hold values from -0.0625 to 0.0625
Outputs:
- mixed: bfloat16 [512, 6144], P(('group', 'expert'), 'tensor'), parts along dimension 0
The draws below stay inside these ranges and needn't reach their ends.
There are 2 independent parts, one for each index of `group`. The reference program is written for one: setup_inputs(seed, part) draws one part's arguments, and reference() takes and returns one part's arrays. A program takes and returns all parts, laid end to end along the dimension named above; an argument that names none is the same for every part. Nothing has to cross between parts.
Inputs may be any that keep to these rules, and one draw needn't show every extreme that they name: `routes`: each row names two different experts.
All inputs are finite; a program needn't handle non-finite values.
Results may differ from the reference program's by a relative error of at most 0.005.
Values may be sent and summed in bfloat16 or wider, within the bound.
A program may use at most 192 MiB of HBM per device.

```python
import math
import jax
import jax.numpy as jnp
import numpy as np

D = 6144
FFW = 8192
TOK_DEV = 128
EXPERTS = 4
TOKENS = 256


def steps_of(stream_key, dims, shards, low, largest):
    level, own = 1.0, jax.random.fold_in(stream_key, 6)
    for dim, blocks in shards:
        heights = jnp.exp(jax.random.uniform(jax.random.fold_in(own, dim), (blocks,), jnp.float32, low / len(shards), largest / len(shards)))
        level = level * jnp.repeat(heights, dims[dim] // blocks).reshape([-1 if axis == dim else 1 for axis in range(len(dims))])
    return level


def routed_block(rng, own, number, rows, number_of, top, bound, slope):
    sequence = jax.random.permutation(rng, number_of)
    packed, usual = shares(number_of, rows * top, bound, slope, True), shares(number_of, rows * top, bound, slope, False)
    places = jnp.arange(number_of)

    def named(tallies, turn):
        used = int((tallies > 0).sum())
        fixed = max(1, used // 4)
        passed = fixed + (places - fixed + turn * (used - fixed)) % max(1, number_of - fixed)
        return jnp.zeros((number_of,), jnp.int32).at[sequence[jnp.where(places < fixed, places, passed)]].set(jnp.asarray(tallies, jnp.int32))

    tallies = jnp.where(number % 4 == 0, named(packed, number // 4), named(usual, number - number // 4 - 1))
    mixed = jax.random.permutation(jax.random.fold_in(own, 3), number_of)
    donor, taker = mixed[0:number_of // 2 * 2:2], mixed[1:number_of // 2 * 2:2]
    margin = jnp.minimum(tallies[donor] - 1, bound - tallies[taker]) // 2
    margin = jnp.where((donor == sequence[0]) | (taker == sequence[0]) | (tallies[taker] == 0), 0, jnp.maximum(margin, 0))
    passed = jax.random.randint(jax.random.fold_in(own, 4), (number_of // 2,), 0, 1 << 20) % (margin + 1)
    tallies = tallies.at[donor].add(-passed).at[taker].add(passed)
    labels = jnp.searchsorted(jnp.cumsum(tallies), jnp.arange(rows * top), side="right").astype(jnp.int32)
    grid = labels.reshape(top, rows).T
    grid = grid[jax.random.permutation(jax.random.fold_in(own, 1), rows)]
    turn = jax.random.randint(jax.random.fold_in(own, 2), (rows, 1), 0, top)
    return jnp.take_along_axis(grid, (jnp.arange(top)[None, :] + turn) % top, axis=1)


def shares(count, total, reach, slope, full):
    weights = [(1 << 20) // math.isqrt(grade ** slope) + 1 for grade in range(1, count + 1)]
    largest = reach if full else min(reach, max(-(-total // count), total * weights[0] // sum(weights)))
    least = 1 if total - largest >= count - 1 else 0
    given, spare = [largest] + [least] * (count - 1), total - largest - least * (count - 1)
    while spare > 0:
        candidates = [i for i in range(1, count) if given[i] < largest] or [i for i in range(1, count) if given[i] < reach]
        pool, left = sum([weights[i] for i in candidates]), spare
        for i in candidates:
            addition = min(reach - given[i], max(1, left * weights[i] // pool), spare)
            given[i] = given[i] + addition
            spare = spare - addition
    return np.array(given)


def centred(stream_key, shape, spread, reach, shards=(), dtype=jnp.bfloat16):
    array = jax.random.normal(stream_key, shape, jnp.float32) * spread
    if len(shards) > 0:
        array = steps_of(stream_key, shape, shards, -0.22, 0.18) * array
    return jnp.clip(array, min=-reach, max=reach).astype(dtype)


def setup_inputs(seed: int = 0, part: int = 0) -> dict:
    key_of = jax.random.split(jax.random.key(seed), 7)
    part_splits = jax.random.split(jax.random.fold_in(key_of[6], part), 7)
    tokens = centred(part_splits[0], (TOKENS, D), 1.0, 6.0, ((0, 2), (1, 8)))
    routes_keys = jax.random.split(jax.random.fold_in(part_splits[1], 1), TOKENS // TOK_DEV)
    routes_turns = jax.random.permutation(jax.random.fold_in(part_splits[1], 3), TOKENS // TOK_DEV)
    routes = jax.vmap(lambda own, number: routed_block(jax.random.fold_in(part_splits[1], 2), own, number, TOK_DEV, EXPERTS, 2, TOK_DEV, 2))(routes_keys, routes_turns).reshape((TOKENS, 2))
    route_weights = jnp.clip(jax.random.uniform(part_splits[2], (TOKENS, 2), jnp.float32, 0.1, 0.9), 0.1, 0.9)
    gate_weight = centred(key_of[3], (EXPERTS, FFW, D), D ** -0.5, 0.078125, ((0, 2), (1, 8)))
    up_weight = centred(key_of[4], (EXPERTS, FFW, D), D ** -0.5, 0.078125, ((0, 2), (1, 8)))
    down_weight = centred(key_of[5], (EXPERTS, D, FFW), FFW ** -0.5, 0.0625, ((0, 2), (1, 8)))
    return {"tokens": tokens, "routes": routes, "route_weights": route_weights, "gate_weight": gate_weight, "up_weight": up_weight, "down_weight": down_weight}


def reference(tokens, routes, route_weights, gate_weight, up_weight, down_weight):
    total = jnp.zeros((tokens.shape[0], tokens.shape[1]), jnp.float32)
    for expert in range(EXPERTS):
        gate = jnp.dot(tokens, gate_weight[expert].T, preferred_element_type=jnp.float32)
        up = jnp.dot(tokens, up_weight[expert].T, preferred_element_type=jnp.float32)
        hidden = (jax.nn.silu(gate) * up).astype(jnp.bfloat16)
        result = jnp.dot(hidden, down_weight[expert].T, preferred_element_type=jnp.float32)
        factor = jnp.sum(jnp.where(routes == expert, route_weights, jnp.float32(0.0)), axis=1)
        total = total + factor[:, None] * result
    return total.astype(jnp.bfloat16)
```

```python
import functools
import jax
import jax.numpy as jnp
from jax import lax
from jax.experimental import pallas as pl
from jax.experimental.pallas import tpu as pltpu
from jax.sharding import PartitionSpec as P

MESH = pl.DeviceIdType.MESH
F32 = jnp.float32
BF16 = jnp.bfloat16
SLOTS = 3


def positions(block_routes, experts, capacity):
    hits = (block_routes[:, :, None] == jnp.arange(experts, dtype=jnp.int32)[None, None, :]).astype(
        jnp.int32
    )
    per_token = jnp.sum(hits, axis=1)
    before = jnp.cumsum(per_token, axis=0) - per_token
    slot = jnp.sum(hits * before[:, None, :], axis=2)
    return block_routes * capacity + slot


def general(tokens, routes, route_weights, gate_weight, up_weight, down_weight):
    exp_dev = gate_weight.shape[0]
    owners = lax.axis_size("expert")
    experts = exp_dev * owners
    rows = routes.shape[0] // owners
    slots_all = experts * rows
    owner_id = lax.axis_index("expert")
    blocks = routes.reshape(owners, rows, 2)
    flat = jax.vmap(positions, (0, None, None))(blocks, experts, rows)
    own_flat = lax.dynamic_index_in_dim(flat, owner_id, 0, keepdims=False)
    slot_ids = jnp.arange(slots_all, dtype=jnp.int32)
    picker = jnp.sum(
        (slot_ids[:, None, None] == own_flat[None, :, :]).astype(jnp.float32), axis=2
    ).astype(jnp.bfloat16)
    features = lax.all_gather(tokens, "tensor", axis=1, tiled=True)
    packed = jnp.dot(picker, features, preferred_element_type=jnp.float32).astype(jnp.bfloat16)
    packed = packed.reshape(owners, exp_dev, rows, features.shape[1])
    arrived = lax.all_to_all(packed, "expert", split_axis=0, concat_axis=2, tiled=True)[0]
    gate = jnp.einsum("esd,ehd->esh", arrived, gate_weight, preferred_element_type=jnp.float32)
    up = jnp.einsum("esd,ehd->esh", arrived, up_weight, preferred_element_type=jnp.float32)
    hidden = (jax.nn.silu(gate) * up).astype(jnp.bfloat16)
    d_local = down_weight.shape[1]
    result = jnp.einsum(
        "esf,edf->esd",
        lax.all_gather(hidden, "tensor", axis=2, tiled=True),
        down_weight,
        preferred_element_type=jnp.float32,
    )
    weight_blocks = route_weights.reshape(owners, rows, 2)
    matches = slot_ids[None, None, :, None] == flat[:, :, None, :]
    mixer_all = jnp.sum(jnp.where(matches, weight_blocks[:, :, None, :], jnp.float32(0.0)), axis=3)
    parts = result.reshape(exp_dev, owners, rows, d_local)
    returned = lax.all_to_all(parts, "expert", split_axis=1, concat_axis=0, tiled=True)
    mixer = lax.dynamic_index_in_dim(mixer_all, owner_id, 0, keepdims=False)
    mixed = jnp.dot(
        mixer,
        returned.reshape(slots_all, d_local),
        precision=lax.Precision.HIGHEST,
        preferred_element_type=jnp.float32,
    )
    return mixed.astype(jnp.bfloat16)


def dot_t(a, b):
    return lax.dot_general(a, b, (((1,), (1,)), ((), ())), preferred_element_type=F32)


def ring_kernel(
    tok_ref, routes_ref, rw_ref, gate_ref, up_ref, down_ref, out_ref,
    xbuf, wbuf, dbuf, acc, hbuf, sown, pbuf, qbuf, sbuf, racc, cbuf, ebuf,
    wsem, dsem, ring_send, ring_recv, sis_send, sis_recv, pq_send, pq_recv, fin_send, fin_recv,
):
    g = lax.axis_index("group")
    c = lax.axis_index("expert")
    t = lax.axis_index("tensor")
    n = 8
    half = n // 2
    dl = tok_ref.shape[1]
    ul = gate_ref.shape[1]
    uh = ul // 2
    rows = routes_ref.shape[0]

    tx = t % 2
    pos = (t // 2) * (1 - tx) + (n - 1 - t // 2) * tx

    def tid(p):
        p = (p + n) % n
        px = p // half
        return 2 * (p * (1 - px) + (n - 1 - p) * px) + px

    def origin(seq):
        if seq == 0:
            return tid(pos)
        d = (seq + 1) // 2
        return tid(pos - d if seq % 2 else pos + d)

    right, left = tid(pos + 1), tid(pos - 1)
    to = ((g, c, right), (g, c, left))
    sister = (g, 1 - c, t)

    def seq_of(way, d):
        return n - 1 if d == half else 2 * d - 1 + way

    def w_copies(seq):
        cols = pl.ds(pl.multiple_of(origin(seq) * dl, 128), dl)
        s = seq % SLOTS
        return [
            pltpu.make_async_copy(ref.at[:, :, cols], wbuf.at[s, i], wsem.at[s, i])
            for i, ref in enumerate((gate_ref, up_ref))
        ]

    def d_copy(seq):
        cols = pl.ds(pl.multiple_of(origin(seq) * ul, 128), ul)
        return pltpu.make_async_copy(down_ref.at[:, :, cols], dbuf.at[seq], dsem.at[seq])

    for seq in range(SLOTS):
        for cp in w_copies(seq):
            cp.start()

    xbuf[0, pl.ds(c, 1)] = tok_ref[...].reshape(1, 2, rows // 4, dl)

    barrier = pltpu.get_barrier_semaphore()
    for dev in (to[0], to[1], sister):
        pl.semaphore_signal(barrier, inc=1, device_id=dev, device_id_type=MESH)
    pl.semaphore_wait(barrier, 3)

    def place(phase, seq, h):
        if phase == 0:
            return xbuf.at[seq, c, h]
        return sown.at[h] if seq == 0 else sbuf.at[seq - 1, c, h]

    def ring_copy(phase, way, d, h):
        src = place(phase, 0 if d == 1 else seq_of(way, d - 1), h)
        return pltpu.make_async_remote_copy(
            src_ref=src, dst_ref=place(phase, seq_of(way, d), h),
            send_sem=ring_send.at[phase, way, d - 1, h], recv_sem=ring_recv.at[phase, way, d - 1, h],
            device_id=to[way], device_id_type=MESH,
        )

    def sis_copy(phase, seq, h):
        ref = place(phase, seq, h)
        return pltpu.make_async_remote_copy(
            src_ref=ref, dst_ref=ref,
            send_sem=sis_send.at[phase, seq, h], recv_sem=sis_recv.at[phase, seq, h],
            device_id=sister, device_id_type=MESH,
        )

    def sis_wait(phase, seq, h):
        ref = xbuf.at[seq, 1 - c, h] if phase == 0 else sbuf.at[seq - 1, 1 - c, h]
        pltpu.make_async_remote_copy(
            src_ref=ref, dst_ref=ref,
            send_sem=sis_send.at[phase, seq, h], recv_sem=sis_recv.at[phase, seq, h],
            device_id=sister, device_id_type=MESH,
        ).wait_recv()

    pending = []

    def start(cp):
        cp.start()
        pending.append(cp)

    def travels(d, way, h):
        return d < half or (d == half and h == way)

    def arrive(phase, d, h, way):
        ring_copy(phase, way, d, h).wait_recv()
        if d < half and travels(d + 1, way, h):
            start(ring_copy(phase, way, d + 1, h))
        start(sis_copy(phase, seq_of(way, d), h))

    def gate_up_half(seq, h):
        s = seq % SLOTS

        def body(i, carry):
            gu, e = i // 2, i % 2
            x = xbuf[seq].reshape(rows, dl)
            r = dot_t(x, wbuf[s, gu, e, h * uh:(h + 1) * uh, :])
            if seq == 0:
                acc[gu, e, h] = r
            else:
                acc[gu, e, h] += r
            return carry

        lax.fori_loop(0, 4, body, 0)

    def w_wait(seq):
        for cp in w_copies(seq):
            cp.wait()

    def gate_up(seq):
        for h in range(2):
            sis_wait(0, seq, h)
        w_wait(seq)
        for h in range(2):
            gate_up_half(seq, h)
        if seq + SLOTS < n:
            for cp in w_copies(seq + SLOTS):
                cp.start()
        if seq + SLOTS == n - 1:
            for q in range(n):
                d_copy(q).start()

    for h in range(2):
        for way in range(2):
            start(ring_copy(0, way, 1, h))
        start(sis_copy(0, 0, h))
    gate_up(0)
    for d in range(1, half):
        for h in range(2):
            for way in range(2):
                arrive(0, d, h, way)
        for way in range(2):
            gate_up(seq_of(way, d))
    for h in range(2):
        arrive(0, half, h, h)
    for h in range(2):
        sis_wait(0, n - 1, h)
    w_wait(n - 1)

    r0, r1 = routes_ref[:, 0:1], routes_ref[:, 1:2]
    mine = jnp.where(c == 0, r0, r1)
    other = jnp.where(c == 0, r1, r0)

    def hidden(h):
        hs = []
        for e in range(2):
            v = acc[0, e, h]
            hs.append(v / (1.0 + jnp.exp(-v)) * acc[1, e, h])
        pbuf[h] = jnp.where(other == 2 * c, hs[0], hs[1]).astype(BF16)
        sown[h] = jnp.where(mine == 2 * c, hs[0], hs[1]).astype(BF16)
        for e in range(2):
            hbuf[e, h] = hs[e].astype(BF16)

    def pq_copy(h):
        return pltpu.make_async_remote_copy(
            src_ref=pbuf.at[h], dst_ref=qbuf.at[h], send_sem=pq_send.at[h], recv_sem=pq_recv.at[h],
            device_id=sister, device_id_type=MESH,
        )

    def merge(h):
        pq_copy(h).wait_recv()
        sown[h] = jnp.where(mine // 2 == c, sown[h].astype(F32), qbuf[h].astype(F32)).astype(BF16)
        for way in range(2):
            start(ring_copy(1, way, 1, h))

    def down(seq, h):
        def body(e, carry):
            if seq == 0:
                a = hbuf[e, h]
            else:
                a = jnp.where(r0 == 2 * c + e, sbuf[seq - 1, 0, h].astype(F32), sbuf[seq - 1, 1, h].astype(F32)).astype(BF16)
            r = dot_t(a, dbuf[seq, e, :, h * uh:(h + 1) * uh])
            if seq == 0 and h == 0:
                racc[e] = r
            else:
                racc[e] += r
            return carry

        lax.fori_loop(0, 2, body, 0)

    gate_up_half(n - 1, 0)
    hidden(0)
    start(pq_copy(0))
    gate_up_half(n - 1, 1)
    merge(0)
    hidden(1)
    start(pq_copy(1))
    d_copy(0).wait()
    down(0, 0)
    merge(1)
    down(0, 1)
    for d in range(1, half + 1):
        for h in range(2):
            ways = [way for way in range(2) if travels(d, way, h)]
            for way in ways:
                arrive(1, d, h, way)
            for way in ways:
                seq = seq_of(way, d)
                if h == 0:
                    d_copy(seq).wait()
                sis_wait(1, seq, h)
                down(seq, h)

    w0, w1 = rw_ref[:, 0:1], rw_ref[:, 1:2]
    zero = jnp.zeros_like(w0)
    total = None
    for e in range(2):
        f = jnp.where(r0 == 2 * c + e, w0, zero) + jnp.where(r1 == 2 * c + e, w1, zero)
        term = f * racc[e]
        total = term if total is None else total + term
    cbuf[...] = total.reshape(2, rows // 2, dl)
    fin = pltpu.make_async_remote_copy(
        src_ref=cbuf.at[1 - c], dst_ref=ebuf, send_sem=fin_send, recv_sem=fin_recv,
        device_id=sister, device_id_type=MESH,
    )
    start(fin)
    fin.wait_recv()
    out_ref[...] = (cbuf[c] + ebuf[...]).astype(BF16)
    for cp in pending:
        cp.wait_send()


def fused(tokens, routes, route_weights, gate_weight, up_weight, down_weight):
    n = 8
    rows, dl = routes.shape[0], tokens.shape[1]
    ul, uh = gate_weight.shape[1], gate_weight.shape[1] // 2
    vmem = pl.BlockSpec(memory_space=pltpu.VMEM)
    hbm = pl.BlockSpec(memory_space=pl.ANY)
    dma = pltpu.SemaphoreType.DMA
    flops = 2 * 2 * rows * ul * dl * n * 3
    moved = 2 * (gate_weight.size + up_weight.size + down_weight.size)
    return pl.pallas_call(
        ring_kernel,
        out_shape=jax.ShapeDtypeStruct(tokens.shape, BF16),
        in_specs=[vmem, vmem, vmem, hbm, hbm, hbm],
        out_specs=vmem,
        scratch_shapes=[
            pltpu.VMEM((n, 2, 2, rows // 4, dl), BF16),
            pltpu.VMEM((SLOTS, 2, 2, ul, dl), BF16),
            pltpu.VMEM((n, 2, dl, ul), BF16),
            pltpu.VMEM((2, 2, 2, rows, uh), F32),
            pltpu.VMEM((2, 2, rows, uh), BF16),
            pltpu.VMEM((2, rows, uh), BF16),
            pltpu.VMEM((2, rows, uh), BF16),
            pltpu.VMEM((2, rows, uh), BF16),
            pltpu.VMEM((n - 1, 2, 2, rows, uh), BF16),
            pltpu.VMEM((2, rows, dl), F32),
            pltpu.VMEM((2, rows // 2, dl), F32),
            pltpu.VMEM((rows // 2, dl), F32),
            dma((SLOTS, 2)), dma((n,)),
            dma((2, 2, n // 2, 2)), dma((2, 2, n // 2, 2)),
            dma((2, n, 2)), dma((2, n, 2)),
            dma((2,)), dma((2,)), dma, dma,
        ],
        compiler_params=pltpu.CompilerParams(
            collective_id=0, has_side_effects=True, vmem_limit_bytes=64 * 1024 * 1024 - 256 * 1024
        ),
        cost_estimate=pl.CostEstimate(flops=flops, bytes_accessed=moved, transcendentals=4 * rows * ul),
    )(tokens, routes, route_weights, gate_weight, up_weight, down_weight)


def solution(mesh):
    placed = (
        P(("group", "expert"), "tensor"),
        P("group", None),
        P("group", None),
        P("expert", "tensor", None),
        P("expert", "tensor", None),
        P("expert", "tensor", None),
    )
    fits = mesh.shape["tensor"] == 8 and mesh.shape["expert"] == 2
    return jax.shard_map(
        fused if fits else general,
        mesh=mesh,
        in_specs=placed,
        out_specs=P(("group", "expert"), "tensor"),
        check_vma=False,
    )
```

```python
import functools
import jax
import jax.numpy as jnp
from jax import lax
from jax.experimental import pallas as pl
from jax.experimental.pallas import tpu as pltpu
from jax.sharding import PartitionSpec as P

MESH = pl.DeviceIdType.MESH
F32 = jnp.float32
BF16 = jnp.bfloat16
SLOTS = 3


def positions(block_routes, experts, capacity):
    hits = (block_routes[:, :, None] == jnp.arange(experts, dtype=jnp.int32)[None, None, :]).astype(
        jnp.int32
    )
    per_token = jnp.sum(hits, axis=1)
    before = jnp.cumsum(per_token, axis=0) - per_token
    slot = jnp.sum(hits * before[:, None, :], axis=2)
    return block_routes * capacity + slot


def general(tokens, routes, route_weights, gate_weight, up_weight, down_weight):
    exp_dev = gate_weight.shape[0]
    owners = lax.axis_size("expert")
    experts = exp_dev * owners
    rows = routes.shape[0] // owners
    slots_all = experts * rows
    owner_id = lax.axis_index("expert")
    blocks = routes.reshape(owners, rows, 2)
    flat = jax.vmap(positions, (0, None, None))(blocks, experts, rows)
    own_flat = lax.dynamic_index_in_dim(flat, owner_id, 0, keepdims=False)
    slot_ids = jnp.arange(slots_all, dtype=jnp.int32)
    picker = jnp.sum(
        (slot_ids[:, None, None] == own_flat[None, :, :]).astype(jnp.float32), axis=2
    ).astype(jnp.bfloat16)
    features = lax.all_gather(tokens, "tensor", axis=1, tiled=True)
    packed = jnp.dot(picker, features, preferred_element_type=jnp.float32).astype(jnp.bfloat16)
    packed = packed.reshape(owners, exp_dev, rows, features.shape[1])
    arrived = lax.all_to_all(packed, "expert", split_axis=0, concat_axis=2, tiled=True)[0]
    gate = jnp.einsum("esd,ehd->esh", arrived, gate_weight, preferred_element_type=jnp.float32)
    up = jnp.einsum("esd,ehd->esh", arrived, up_weight, preferred_element_type=jnp.float32)
    hidden = (jax.nn.silu(gate) * up).astype(jnp.bfloat16)
    d_local = down_weight.shape[1]
    result = jnp.einsum(
        "esf,edf->esd",
        lax.all_gather(hidden, "tensor", axis=2, tiled=True),
        down_weight,
        preferred_element_type=jnp.float32,
    )
    weight_blocks = route_weights.reshape(owners, rows, 2)
    matches = slot_ids[None, None, :, None] == flat[:, :, None, :]
    mixer_all = jnp.sum(jnp.where(matches, weight_blocks[:, :, None, :], jnp.float32(0.0)), axis=3)
    parts = result.reshape(exp_dev, owners, rows, d_local)
    returned = lax.all_to_all(parts, "expert", split_axis=1, concat_axis=0, tiled=True)
    mixer = lax.dynamic_index_in_dim(mixer_all, owner_id, 0, keepdims=False)
    mixed = jnp.dot(
        mixer,
        returned.reshape(slots_all, d_local),
        precision=lax.Precision.HIGHEST,
        preferred_element_type=jnp.float32,
    )
    return mixed.astype(jnp.bfloat16)


def dot_t(a, b):
    return lax.dot_general(a, b, (((1,), (1,)), ((), ())), preferred_element_type=F32)


def ring_kernel(
    tok_ref, routes_ref, rw_ref, gate_ref, up_ref, down_ref, out_ref,
    xbuf, wbuf, dbuf, acc, hbuf, sown, pbuf, qbuf, sbuf, racc, cbuf, ebuf,
    wsem, dsem, ring_send, ring_recv, sis_send, sis_recv, pq_send, pq_recv, fin_send, fin_recv,
):
    g = lax.axis_index("group")
    c = lax.axis_index("expert")
    t = lax.axis_index("tensor")
    n = 8
    half = n // 2
    dl = tok_ref.shape[1]
    ul = gate_ref.shape[1]
    uh = ul // 2
    rows = routes_ref.shape[1]

    tx = t % 2
    pos = (t // 2) * (1 - tx) + (n - 1 - t // 2) * tx

    def tid(p):
        p = (p + n) % n
        px = p // half
        return 2 * (p * (1 - px) + (n - 1 - p) * px) + px

    def origin(seq):
        if seq == 0:
            return tid(pos)
        d = (seq + 1) // 2
        return tid(pos - d if seq % 2 else pos + d)

    right, left = tid(pos + 1), tid(pos - 1)
    to = ((g, c, right), (g, c, left))
    sister = (g, 1 - c, t)

    def seq_of(way, d):
        return n - 1 if d == half else 2 * d - 1 + way

    def w_copies(seq):
        cols = pl.ds(pl.multiple_of(origin(seq) * dl, 128), dl)
        s = seq % SLOTS
        return [
            pltpu.make_async_copy(ref.at[:, :, cols], wbuf.at[s, i], wsem.at[s, i])
            for i, ref in enumerate((gate_ref, up_ref))
        ]

    def d_copy(seq):
        cols = pl.ds(pl.multiple_of(origin(seq) * ul, 128), ul)
        return pltpu.make_async_copy(down_ref.at[:, :, cols], dbuf.at[seq], dsem.at[seq])

    for cp in w_copies(0):
        cp.start()

    xbuf[0, pl.ds(c, 1)] = tok_ref[...].reshape(1, 2, rows // 4, dl)

    barrier = pltpu.get_barrier_semaphore()
    for dev in (to[0], to[1], sister):
        pl.semaphore_signal(barrier, inc=1, device_id=dev, device_id_type=MESH)
    pl.semaphore_wait(barrier, 3)

    def place(phase, seq, h):
        if phase == 0:
            return xbuf.at[seq, c, h]
        return sown.at[h] if seq == 0 else sbuf.at[seq - 1, c, h]

    def ring_copy(phase, way, d, h):
        src = place(phase, 0 if d == 1 else seq_of(way, d - 1), h)
        return pltpu.make_async_remote_copy(
            src_ref=src, dst_ref=place(phase, seq_of(way, d), h),
            send_sem=ring_send.at[phase, way, d - 1, h], recv_sem=ring_recv.at[phase, way, d - 1, h],
            device_id=to[way], device_id_type=MESH,
        )

    def sis_copy(phase, seq, h):
        ref = place(phase, seq, h)
        return pltpu.make_async_remote_copy(
            src_ref=ref, dst_ref=ref,
            send_sem=sis_send.at[phase, seq, h], recv_sem=sis_recv.at[phase, seq, h],
            device_id=sister, device_id_type=MESH,
        )

    def sis_wait(phase, seq, h):
        ref = xbuf.at[seq, 1 - c, h] if phase == 0 else sbuf.at[seq - 1, 1 - c, h]
        pltpu.make_async_remote_copy(
            src_ref=ref, dst_ref=ref,
            send_sem=sis_send.at[phase, seq, h], recv_sem=sis_recv.at[phase, seq, h],
            device_id=sister, device_id_type=MESH,
        ).wait_recv()

    pending = []

    def start(cp):
        cp.start()
        pending.append(cp)

    def travels(d, way, h):
        return d < half or (d == half and h == way)

    def arrive(phase, d, h, way):
        ring_copy(phase, way, d, h).wait_recv()
        if d < half and travels(d + 1, way, h):
            start(ring_copy(phase, way, d + 1, h))
        start(sis_copy(phase, seq_of(way, d), h))

    def gate_up_half(seq, h):
        s = seq % SLOTS

        def body(i, carry):
            gu, e = i // 2, i % 2
            x = xbuf[seq].reshape(rows, dl)
            r = dot_t(wbuf[s, gu, e, h * uh:(h + 1) * uh, :], x)
            if seq == 0:
                acc[gu, e, h] = r
            else:
                acc[gu, e, h] += r
            return carry

        lax.fori_loop(0, 4, body, 0)

    def w_wait(seq):
        for cp in w_copies(seq):
            cp.wait()

    def gate_up(seq):
        for h in range(2):
            sis_wait(0, seq, h)
        w_wait(seq)
        for h in range(2):
            gate_up_half(seq, h)
        if seq + SLOTS < n:
            for cp in w_copies(seq + SLOTS):
                cp.start()

    for h in range(2):
        for way in range(2):
            start(ring_copy(0, way, 1, h))
        start(sis_copy(0, 0, h))
    for seq in range(1, SLOTS):
        for cp in w_copies(seq):
            cp.start()
    for d in range(1, half):
        for h in range(2):
            for way in range(2):
                arrive(0, d, h, way)
            gate_up(2 * (d - 1) + h)
    for h in range(2):
        arrive(0, half, h, h)
    gate_up(n - 2)
    for h in range(2):
        sis_wait(0, n - 1, h)
    w_wait(n - 1)
    for seq in range(n):
        d_copy(seq).start()

    r0, r1 = routes_ref[0:1, :], routes_ref[1:2, :]
    mine = jnp.where(c == 0, r0, r1)
    other = jnp.where(c == 0, r1, r0)

    def hidden(h):
        hs = []
        for e in range(2):
            v = acc[0, e, h]
            hs.append(v / (1.0 + jnp.exp(-v)) * acc[1, e, h])
        pbuf[h] = jnp.where(other == 2 * c, hs[0], hs[1]).astype(BF16)
        sown[h] = jnp.where(mine == 2 * c, hs[0], hs[1]).astype(BF16)
        for e in range(2):
            hbuf[e, h] = hs[e].astype(BF16)

    def pq_copy(h):
        return pltpu.make_async_remote_copy(
            src_ref=pbuf.at[h], dst_ref=qbuf.at[h], send_sem=pq_send.at[h], recv_sem=pq_recv.at[h],
            device_id=sister, device_id_type=MESH,
        )

    def merge(h):
        pq_copy(h).wait_recv()
        sown[h] = jnp.where(mine // 2 == c, sown[h].astype(F32), qbuf[h].astype(F32)).astype(BF16)
        for way in range(2):
            start(ring_copy(1, way, 1, h))

    def down(seq, h):
        def body(e, carry):
            if seq == 0:
                a = hbuf[e, h]
            else:
                a = jnp.where(r0 == 2 * c + e, sbuf[seq - 1, 0, h].astype(F32), sbuf[seq - 1, 1, h].astype(F32)).astype(BF16)
            r = jnp.dot(dbuf[seq, e, :, h * uh:(h + 1) * uh], a, preferred_element_type=F32)
            if seq == 0 and h == 0:
                racc[e] = r
            else:
                racc[e] += r
            return carry

        lax.fori_loop(0, 2, body, 0)

    gate_up_half(n - 1, 0)
    hidden(0)
    start(pq_copy(0))
    gate_up_half(n - 1, 1)
    merge(0)
    hidden(1)
    start(pq_copy(1))
    d_copy(0).wait()
    down(0, 0)
    merge(1)
    down(0, 1)
    for d in range(1, half + 1):
        for h in range(2):
            ways = [way for way in range(2) if travels(d, way, h)]
            for way in ways:
                arrive(1, d, h, way)
            for way in ways:
                seq = seq_of(way, d)
                if h == 0:
                    d_copy(seq).wait()
                sis_wait(1, seq, h)
                down(seq, h)

    w0, w1 = rw_ref[0:1, :], rw_ref[1:2, :]
    zero = jnp.zeros_like(w0)
    total = None
    for e in range(2):
        f = jnp.where(r0 == 2 * c + e, w0, zero) + jnp.where(r1 == 2 * c + e, w1, zero)
        term = f * racc[e]
        total = term if total is None else total + term
    for q in range(2):
        cbuf[q] = total[:, q * (rows // 2):(q + 1) * (rows // 2)]
    fin = pltpu.make_async_remote_copy(
        src_ref=cbuf.at[1 - c], dst_ref=ebuf, send_sem=fin_send, recv_sem=fin_recv,
        device_id=sister, device_id_type=MESH,
    )
    start(fin)
    fin.wait_recv()
    out_ref[...] = jnp.transpose(cbuf[c] + ebuf[...]).astype(BF16)
    for cp in pending:
        cp.wait_send()


def fused(tokens, routes, route_weights, gate_weight, up_weight, down_weight):
    n = 8
    rows, dl = routes.shape[0], tokens.shape[1]
    ul, uh = gate_weight.shape[1], gate_weight.shape[1] // 2
    vmem = pl.BlockSpec(memory_space=pltpu.VMEM)
    hbm = pl.BlockSpec(memory_space=pl.ANY)
    dma = pltpu.SemaphoreType.DMA
    flops = 2 * 2 * rows * ul * dl * n * 3
    moved = 2 * (gate_weight.size + up_weight.size + down_weight.size)
    return pl.pallas_call(
        ring_kernel,
        out_shape=jax.ShapeDtypeStruct(tokens.shape, BF16),
        in_specs=[vmem, vmem, vmem, hbm, hbm, hbm],
        out_specs=vmem,
        scratch_shapes=[
            pltpu.VMEM((n, 2, 2, rows // 4, dl), BF16),
            pltpu.VMEM((SLOTS, 2, 2, ul, dl), BF16),
            pltpu.VMEM((n, 2, dl, ul), BF16),
            pltpu.VMEM((2, 2, 2, uh, rows), F32),
            pltpu.VMEM((2, 2, uh, rows), BF16),
            pltpu.VMEM((2, uh, rows), BF16),
            pltpu.VMEM((2, uh, rows), BF16),
            pltpu.VMEM((2, uh, rows), BF16),
            pltpu.VMEM((n - 1, 2, 2, uh, rows), BF16),
            pltpu.VMEM((2, dl, rows), F32),
            pltpu.VMEM((2, dl, rows // 2), F32),
            pltpu.VMEM((dl, rows // 2), F32),
            dma((SLOTS, 2)), dma((n,)),
            dma((2, 2, n // 2, 2)), dma((2, 2, n // 2, 2)),
            dma((2, n, 2)), dma((2, n, 2)),
            dma((2,)), dma((2,)), dma, dma,
        ],
        compiler_params=pltpu.CompilerParams(
            collective_id=0, has_side_effects=True, vmem_limit_bytes=64 * 1024 * 1024 - 256 * 1024
        ),
        cost_estimate=pl.CostEstimate(flops=flops, bytes_accessed=moved, transcendentals=4 * rows * ul),
    )(tokens, routes.T, route_weights.T, gate_weight, up_weight, down_weight)


def solution(mesh):
    placed = (
        P(("group", "expert"), "tensor"),
        P("group", None),
        P("group", None),
        P("expert", "tensor", None),
        P("expert", "tensor", None),
        P("expert", "tensor", None),
    )
    fits = mesh.shape["tensor"] == 8 and mesh.shape["expert"] == 2
    return jax.shard_map(
        fused if fits else general,
        mesh=mesh,
        in_specs=placed,
        out_specs=P(("group", "expert"), "tensor"),
        check_vma=False,
    )
```

```python
import functools
import jax
import jax.numpy as jnp
from jax import lax
from jax.experimental import pallas as pl
from jax.experimental.pallas import tpu as pltpu
from jax.sharding import PartitionSpec as P

MESH = pl.DeviceIdType.MESH
F32 = jnp.float32
BF16 = jnp.bfloat16
SLOTS = 3


def positions(block_routes, experts, capacity):
    hits = (block_routes[:, :, None] == jnp.arange(experts, dtype=jnp.int32)[None, None, :]).astype(
        jnp.int32
    )
    per_token = jnp.sum(hits, axis=1)
    before = jnp.cumsum(per_token, axis=0) - per_token
    slot = jnp.sum(hits * before[:, None, :], axis=2)
    return block_routes * capacity + slot


def general(tokens, routes, route_weights, gate_weight, up_weight, down_weight):
    exp_dev = gate_weight.shape[0]
    owners = lax.axis_size("expert")
    experts = exp_dev * owners
    rows = routes.shape[0] // owners
    slots_all = experts * rows
    owner_id = lax.axis_index("expert")
    blocks = routes.reshape(owners, rows, 2)
    flat = jax.vmap(positions, (0, None, None))(blocks, experts, rows)
    own_flat = lax.dynamic_index_in_dim(flat, owner_id, 0, keepdims=False)
    slot_ids = jnp.arange(slots_all, dtype=jnp.int32)
    picker = jnp.sum(
        (slot_ids[:, None, None] == own_flat[None, :, :]).astype(jnp.float32), axis=2
    ).astype(jnp.bfloat16)
    features = lax.all_gather(tokens, "tensor", axis=1, tiled=True)
    packed = jnp.dot(picker, features, preferred_element_type=jnp.float32).astype(jnp.bfloat16)
    packed = packed.reshape(owners, exp_dev, rows, features.shape[1])
    arrived = lax.all_to_all(packed, "expert", split_axis=0, concat_axis=2, tiled=True)[0]
    gate = jnp.einsum("esd,ehd->esh", arrived, gate_weight, preferred_element_type=jnp.float32)
    up = jnp.einsum("esd,ehd->esh", arrived, up_weight, preferred_element_type=jnp.float32)
    hidden = (jax.nn.silu(gate) * up).astype(jnp.bfloat16)
    d_local = down_weight.shape[1]
    result = jnp.einsum(
        "esf,edf->esd",
        lax.all_gather(hidden, "tensor", axis=2, tiled=True),
        down_weight,
        preferred_element_type=jnp.float32,
    )
    weight_blocks = route_weights.reshape(owners, rows, 2)
    matches = slot_ids[None, None, :, None] == flat[:, :, None, :]
    mixer_all = jnp.sum(jnp.where(matches, weight_blocks[:, :, None, :], jnp.float32(0.0)), axis=3)
    parts = result.reshape(exp_dev, owners, rows, d_local)
    returned = lax.all_to_all(parts, "expert", split_axis=1, concat_axis=0, tiled=True)
    mixer = lax.dynamic_index_in_dim(mixer_all, owner_id, 0, keepdims=False)
    mixed = jnp.dot(
        mixer,
        returned.reshape(slots_all, d_local),
        precision=lax.Precision.HIGHEST,
        preferred_element_type=jnp.float32,
    )
    return mixed.astype(jnp.bfloat16)


def dot_t(a, b):
    return lax.dot_general(a, b, (((1,), (1,)), ((), ())), preferred_element_type=F32)


def ring_kernel(
    tok_ref, routes_ref, rw_ref, gate_ref, up_ref, down_ref, out_ref,
    xbuf, wbuf, dbuf, acc, hbuf, sown, pbuf, qbuf, sbuf, racc, cbuf, ebuf,
    wsem, dsem, ring_send, ring_recv, sis_send, sis_recv, pq_send, pq_recv, fin_send, fin_recv,
):
    g = lax.axis_index("group")
    c = lax.axis_index("expert")
    t = lax.axis_index("tensor")
    n = 8
    half = n // 2
    dl = tok_ref.shape[1]
    ul = gate_ref.shape[1]
    uh = ul // 2
    rows = routes_ref.shape[1]

    tx = t % 2
    pos = (t // 2) * (1 - tx) + (n - 1 - t // 2) * tx

    def tid(p):
        p = (p + n) % n
        px = p // half
        return 2 * (p * (1 - px) + (n - 1 - p) * px) + px

    def origin(seq):
        if seq == 0:
            return tid(pos)
        d = (seq + 1) // 2
        return tid(pos - d if seq % 2 else pos + d)

    right, left = tid(pos + 1), tid(pos - 1)
    to = ((g, c, right), (g, c, left))
    sister = (g, 1 - c, t)

    def seq_of(way, d):
        return n - 1 if d == half else 2 * d - 1 + way

    def w_copies(seq):
        cols = pl.ds(pl.multiple_of(origin(seq) * dl, 128), dl)
        s = seq % SLOTS
        return [
            pltpu.make_async_copy(ref.at[:, :, cols], wbuf.at[s, i], wsem.at[s, i])
            for i, ref in enumerate((gate_ref, up_ref))
        ]

    def d_copy(seq):
        cols = pl.ds(pl.multiple_of(origin(seq) * ul, 128), ul)
        return pltpu.make_async_copy(down_ref.at[:, :, cols], dbuf.at[seq], dsem.at[seq])

    for cp in w_copies(0):
        cp.start()

    xbuf[0, pl.ds(c, 1)] = tok_ref[...].reshape(1, 2, rows // 4, dl)

    barrier = pltpu.get_barrier_semaphore()
    for dev in (to[0], to[1], sister):
        pl.semaphore_signal(barrier, inc=1, device_id=dev, device_id_type=MESH)
    pl.semaphore_wait(barrier, 3)

    def place(phase, seq, h):
        if phase == 0:
            return xbuf.at[seq, c, h]
        return sown.at[h] if seq == 0 else sbuf.at[seq - 1, c, h]

    def ring_copy(phase, way, d, h):
        src = place(phase, 0 if d == 1 else seq_of(way, d - 1), h)
        return pltpu.make_async_remote_copy(
            src_ref=src, dst_ref=place(phase, seq_of(way, d), h),
            send_sem=ring_send.at[phase, way, d - 1, h], recv_sem=ring_recv.at[phase, way, d - 1, h],
            device_id=to[way], device_id_type=MESH,
        )

    def sis_copy(phase, seq, h):
        ref = place(phase, seq, h)
        return pltpu.make_async_remote_copy(
            src_ref=ref, dst_ref=ref,
            send_sem=sis_send.at[phase, seq, h], recv_sem=sis_recv.at[phase, seq, h],
            device_id=sister, device_id_type=MESH,
        )

    def sis_wait(phase, seq, h):
        ref = xbuf.at[seq, 1 - c, h] if phase == 0 else sbuf.at[seq - 1, 1 - c, h]
        pltpu.make_async_remote_copy(
            src_ref=ref, dst_ref=ref,
            send_sem=sis_send.at[phase, seq, h], recv_sem=sis_recv.at[phase, seq, h],
            device_id=sister, device_id_type=MESH,
        ).wait_recv()

    pending = []

    def start(cp):
        cp.start()
        pending.append(cp)

    def travels(d, way, h):
        return d < half or (d == half and h == way)

    def arrive(phase, d, h, way):
        ring_copy(phase, way, d, h).wait_recv()
        if d < half and travels(d + 1, way, h):
            start(ring_copy(phase, way, d + 1, h))
        start(sis_copy(phase, seq_of(way, d), h))

    def gate_up_half(seq, h):
        s = seq % SLOTS

        def body(i, carry):
            gu, e = i // 2, i % 2
            x = xbuf[seq].reshape(rows, dl)
            r = dot_t(wbuf[s, gu, e, h * uh:(h + 1) * uh, :], x)
            if seq == 0:
                acc[gu, e, h] = r
            else:
                acc[gu, e, h] += r
            return carry

        lax.fori_loop(0, 4, body, 0)

    def w_wait(seq):
        for cp in w_copies(seq):
            cp.wait()

    def gate_up(seq):
        for h in range(2):
            sis_wait(0, seq, h)
        w_wait(seq)
        s = seq % SLOTS

        def body(i, carry):
            gu, e = i // 2, i % 2
            r = dot_t(wbuf[s, gu, e], xbuf[seq].reshape(rows, dl)).reshape(2, uh, rows)
            if seq == 0:
                acc[gu, e] = r
            else:
                acc[gu, e] += r
            return carry

        lax.fori_loop(0, 4, body, 0)
        if seq + SLOTS < n:
            for cp in w_copies(seq + SLOTS):
                cp.start()

    for h in range(2):
        for way in range(2):
            start(ring_copy(0, way, 1, h))
        start(sis_copy(0, 0, h))
    for seq in range(1, SLOTS):
        for cp in w_copies(seq):
            cp.start()
    for d in range(1, half):
        for h in range(2):
            for way in range(2):
                arrive(0, d, h, way)
            gate_up(2 * (d - 1) + h)
    for h in range(2):
        arrive(0, half, h, h)
    gate_up(n - 2)
    for h in range(2):
        sis_wait(0, n - 1, h)
    w_wait(n - 1)
    for seq in range(n):
        d_copy(seq).start()

    r0, r1 = routes_ref[0:1, :], routes_ref[1:2, :]
    mine = jnp.where(c == 0, r0, r1)
    other = jnp.where(c == 0, r1, r0)

    def hidden(h):
        hs = []
        for e in range(2):
            v = acc[0, e, h]
            hs.append(v / (1.0 + jnp.exp(-v)) * acc[1, e, h])
        pbuf[h] = jnp.where(other == 2 * c, hs[0], hs[1]).astype(BF16)
        sown[h] = jnp.where(mine == 2 * c, hs[0], hs[1]).astype(BF16)
        for e in range(2):
            hbuf[e, h] = hs[e].astype(BF16)

    def pq_copy(h):
        return pltpu.make_async_remote_copy(
            src_ref=pbuf.at[h], dst_ref=qbuf.at[h], send_sem=pq_send.at[h], recv_sem=pq_recv.at[h],
            device_id=sister, device_id_type=MESH,
        )

    def merge(h):
        pq_copy(h).wait_recv()
        sown[h] = jnp.where(mine // 2 == c, sown[h].astype(F32), qbuf[h].astype(F32)).astype(BF16)
        for way in range(2):
            start(ring_copy(1, way, 1, h))

    def down(seq, h):
        def body(e, carry):
            if seq == 0:
                a = hbuf[e, h]
            else:
                a = jnp.where(r0 == 2 * c + e, sbuf[seq - 1, 0, h].astype(F32), sbuf[seq - 1, 1, h].astype(F32)).astype(BF16)
            r = jnp.dot(dbuf[seq, e, :, h * uh:(h + 1) * uh], a, preferred_element_type=F32)
            if seq == 0 and h == 0:
                racc[e] = r
            else:
                racc[e] += r
            return carry

        lax.fori_loop(0, 2, body, 0)

    gate_up_half(n - 1, 0)
    hidden(0)
    start(pq_copy(0))
    gate_up_half(n - 1, 1)
    merge(0)
    hidden(1)
    start(pq_copy(1))
    d_copy(0).wait()
    down(0, 0)
    merge(1)
    down(0, 1)
    for d in range(1, half + 1):
        for h in range(2):
            ways = [way for way in range(2) if travels(d, way, h)]
            for way in ways:
                arrive(1, d, h, way)
            for way in ways:
                seq = seq_of(way, d)
                if h == 0:
                    d_copy(seq).wait()
                sis_wait(1, seq, h)
                down(seq, h)

    w0, w1 = rw_ref[0:1, :], rw_ref[1:2, :]
    zero = jnp.zeros_like(w0)
    total = None
    for e in range(2):
        f = jnp.where(r0 == 2 * c + e, w0, zero) + jnp.where(r1 == 2 * c + e, w1, zero)
        term = f * racc[e]
        total = term if total is None else total + term
    for q in range(2):
        cbuf[q] = total[:, q * (rows // 2):(q + 1) * (rows // 2)]
    fin = pltpu.make_async_remote_copy(
        src_ref=cbuf.at[1 - c], dst_ref=ebuf, send_sem=fin_send, recv_sem=fin_recv,
        device_id=sister, device_id_type=MESH,
    )
    start(fin)
    fin.wait_recv()
    out_ref[...] = jnp.transpose(cbuf[c] + ebuf[...]).astype(BF16)
    for cp in pending:
        cp.wait_send()


def fused(tokens, routes, route_weights, gate_weight, up_weight, down_weight):
    n = 8
    rows, dl = routes.shape[0], tokens.shape[1]
    ul, uh = gate_weight.shape[1], gate_weight.shape[1] // 2
    vmem = pl.BlockSpec(memory_space=pltpu.VMEM)
    hbm = pl.BlockSpec(memory_space=pl.ANY)
    dma = pltpu.SemaphoreType.DMA
    flops = 2 * 2 * rows * ul * dl * n * 3
    moved = 2 * (gate_weight.size + up_weight.size + down_weight.size)
    return pl.pallas_call(
        ring_kernel,
        out_shape=jax.ShapeDtypeStruct(tokens.shape, BF16),
        in_specs=[vmem, vmem, vmem, hbm, hbm, hbm],
        out_specs=vmem,
        scratch_shapes=[
            pltpu.VMEM((n, 2, 2, rows // 4, dl), BF16),
            pltpu.VMEM((SLOTS, 2, 2, ul, dl), BF16),
            pltpu.VMEM((n, 2, dl, ul), BF16),
            pltpu.VMEM((2, 2, 2, uh, rows), F32),
            pltpu.VMEM((2, 2, uh, rows), BF16),
            pltpu.VMEM((2, uh, rows), BF16),
            pltpu.VMEM((2, uh, rows), BF16),
            pltpu.VMEM((2, uh, rows), BF16),
            pltpu.VMEM((n - 1, 2, 2, uh, rows), BF16),
            pltpu.VMEM((2, dl, rows), F32),
            pltpu.VMEM((2, dl, rows // 2), F32),
            pltpu.VMEM((dl, rows // 2), F32),
            dma((SLOTS, 2)), dma((n,)),
            dma((2, 2, n // 2, 2)), dma((2, 2, n // 2, 2)),
            dma((2, n, 2)), dma((2, n, 2)),
            dma((2,)), dma((2,)), dma, dma,
        ],
        compiler_params=pltpu.CompilerParams(
            collective_id=0, has_side_effects=True, vmem_limit_bytes=64 * 1024 * 1024 - 256 * 1024
        ),
        cost_estimate=pl.CostEstimate(flops=flops, bytes_accessed=moved, transcendentals=4 * rows * ul),
    )(tokens, routes.T, route_weights.T, gate_weight, up_weight, down_weight)


def solution(mesh):
    placed = (
        P(("group", "expert"), "tensor"),
        P("group", None),
        P("group", None),
        P("expert", "tensor", None),
        P("expert", "tensor", None),
        P("expert", "tensor", None),
    )
    fits = mesh.shape["tensor"] == 8 and mesh.shape["expert"] == 2
    return jax.shard_map(
        fused if fits else general,
        mesh=mesh,
        in_specs=placed,
        out_specs=P(("group", "expert"), "tensor"),
        check_vma=False,
    )
```
